32 devices in a mesh: blk: 4 (over y, x), rhs: 8 (over z, core).
Axes of the slice: x: 2, y: 2, z: 4, core: 2. Of those that a mesh axis runs over, the one named last changes fastest.
Arguments:
- factor: bfloat16 [2, 4, 2048, 8192], P(None, 'blk', 'rhs'), as said below
- loads: float32 [2, 4, 2048, 128], P(None, 'blk', 'rhs'), may hold values from -6 to 6
Outputs:
- advanced: float32 [2, 4, 2048, 128], P(None, 'blk', 'rhs')
The draws below stay inside these ranges and needn't reach their ends.
Inputs may be any that keep to these rules, and one draw needn't show every extreme that they name: factor is block lower triangular: F_gk is zero for k > g, and each diagonal block F_kk is lower triangular with diagonal entries of 0.5 to 1.5.
All inputs are finite; a program needn't handle non-finite values.
Results may differ from the reference program's by a relative error of at most 0.002.
Values may be sent and summed in bfloat16 or wider, within the bound.
A program may use at most 64 MiB of HBM per device.

```python
import jax
import jax.numpy as jnp
from jax import lax

BLOCK = 2048
STEPS = 4
ROUNDS = 2
CASES = 128
N_BLK = 4


def draw_factor(key, part):
    width = STEPS * BLOCK
    shape = (ROUNDS, N_BLK, BLOCK, width)
    key_base = jax.random.fold_in(key, 11)
    key_diag = jax.random.fold_in(key, 13)
    base = jax.random.normal(key_base, shape, jnp.float32)
    off = base * (0.7 / width ** 0.5)
    lower = base * (0.6 / BLOCK ** 0.5)
    diagv = jax.random.uniform(key_diag, shape, jnp.float32, 0.5, 1.5)
    blockrow = (jnp.arange(ROUNDS)[:, None] * N_BLK + jnp.arange(N_BLK)[None, :]).reshape(ROUNDS, N_BLK, 1, 1)
    within = jnp.arange(BLOCK).reshape(1, 1, BLOCK, 1)
    column = jnp.arange(width).reshape(1, 1, 1, width)
    colblock = column // BLOCK
    inner = column % BLOCK
    dval = jnp.where(inner == within, diagv, jnp.where(inner < within, lower, 0.0))
    values = jnp.where(colblock < blockrow, off, jnp.where(colblock == blockrow, dval, 0.0))
    return values.astype(jnp.bfloat16)


def level_of(key, dims, pieces, least, high):
    def one(dim, blocks):
        draws = jax.random.uniform(jax.random.fold_in(jax.random.fold_in(key, 6), dim), (blocks,), jnp.float32, least / len(pieces), high / len(pieces))
        return jnp.repeat(jnp.exp(draws), dims[dim] // blocks).reshape((-1,) + (1,) * (len(dims) - dim - 1))

    level = one(*pieces[0])
    for cut in pieces[1:]:
        level = level * one(*cut)
    return level


def scatter_about(key, extent, spread, reach, cuts=(), dtype=jnp.bfloat16):
    drawn = spread * jax.random.normal(key, extent, jnp.float32)
    if cuts:
        drawn = drawn * level_of(key, extent, cuts, -0.22, 0.18)
    return jnp.clip(drawn, -reach, reach).astype(dtype)


def setup_inputs(seed: int = 0) -> dict:
    key_of = jax.random.split(jax.random.key(seed), 3)
    return {
        "factor": draw_factor(jax.random.fold_in(key_of[2], 71), 0),
        "loads": scatter_about(key_of[1], (ROUNDS, N_BLK, BLOCK, CASES), 1.0, 6.0, ((1, 4), (2, 8)), jnp.float32),
    }


def reference(factor, loads):
    blocks = ROUNDS * N_BLK
    rows = factor.reshape(blocks, BLOCK, STEPS * BLOCK)
    work = loads.reshape(blocks, BLOCK, CASES)
    for step in range(STEPS):
        column = rows[:, :, step * BLOCK:(step + 1) * BLOCK]
        solution = jnp.dot(column[step].astype(jnp.float32), work[step], precision=lax.Precision.HIGHEST)
        sent = solution.astype(jnp.bfloat16)
        update = jnp.dot(column.reshape(blocks * BLOCK, BLOCK), sent, preferred_element_type=jnp.float32)
        work = work - update.reshape(blocks, BLOCK, CASES)
        work = work.at[step].set(solution)
    return work.reshape(ROUNDS, N_BLK, BLOCK, CASES)
```

```python
import functools

import jax
import jax.numpy as jnp
from jax import lax
from jax.experimental import pallas as pl
from jax.experimental.pallas import tpu as pltpu
from jax.sharding import PartitionSpec as P

MESH = pl.DeviceIdType.MESH


def kernel(dims, factor, loads, out, held, gathered, solved, load_sem, g_recv, s_recv,
           g_send, gp_send, b_send, s_send, sp_send):
    cycle, places, steps, rounds, share, block, cases = dims
    chips = places // 2
    position = lax.axis_index("blk")
    place = lax.axis_index("rhs")
    chip = place // 2
    core = place % 2
    partner = place + 1 - 2 * core

    def fetch(r, k):
        return pltpu.make_async_copy(
            factor.at[r, :, pl.ds(k * block, block)], held.at[r, k], load_sem.at[r, k])

    for k in range(steps):
        for r in range(rounds):
            fetch(r, k).start()

    barrier = pltpu.get_barrier_semaphore()
    pl.semaphore_signal(barrier, inc=1, device_id={"rhs": partner}, device_id_type=MESH)
    for d in range(1, chips):
        pl.semaphore_signal(barrier, inc=1, device_id={"rhs": (chip + d) % chips * 2 + core},
                            device_id_type=MESH)
    for d in range(1, cycle):
        pl.semaphore_signal(barrier, inc=1, device_id={"blk": (position + d) % cycle},
                            device_id_type=MESH)

    def copy(buffer, recv, k, source, send, device):
        rows = pl.ds(pl.multiple_of(source * share, share), share)
        return pltpu.make_async_remote_copy(
            src_ref=buffer.at[k, rows], dst_ref=buffer.at[k, rows], send_sem=send,
            recv_sem=recv.at[k, source], device_id=device, device_id_type=MESH)

    def arrived(buffer, recv, k, source):
        copy(buffer, recv, k, source, s_send.at[k, 0], {"rhs": partner}).wait_recv()

    def others(order, body):
        for d in order:
            for sign in (1, -1):
                other = chip + sign * d
                pl.when((other >= 0) & (other < chips))(functools.partial(body, other))

    near = range(1, chips)
    far = range(chips - 1, 0, -1)

    def later(body):
        for d in far:
            other = chip + d
            pl.when(other < chips)(functools.partial(body, other))

    def earlier(body):
        for d in near:
            other = chip - d
            pl.when(other >= 0)(functools.partial(body, other))

    def g_out(k, other):
        return copy(gathered, g_recv, k, place, g_send.at[k, other], {"rhs": other * 2 + core})

    def g_pass(k, other):
        return copy(gathered, g_recv, k, other * 2 + core, gp_send.at[k, other], {"rhs": partner})

    def s_out(k, other):
        return copy(solved, s_recv, k, place, s_send.at[k, other], {"rhs": other * 2 + core})

    def s_pass(k, other):
        return copy(solved, s_recv, k, other * 2 + core, sp_send.at[k, other], {"rhs": partner})

    def b_out(k, d):
        return copy(solved, s_recv, k, place, b_send.at[k, d], {"blk": (k % cycle + d) % cycle})

    mine = pl.ds(pl.multiple_of(place * share, share), share)

    def gather_work(k):
        gathered[k, mine] = out[k // cycle].astype(jnp.bfloat16)
        later(lambda other: g_out(k, other).start())
        g_pass(k, chip).start()

    def pair_dot(k, other, value):
        columns = pl.ds(pl.multiple_of(other * 2 * share, 2 * share), 2 * share)
        return jnp.dot(held[k // cycle, k, :, columns], value, preferred_element_type=jnp.float32)

    def pair(k, other):
        return gathered[k, pl.ds(pl.multiple_of(other * 2 * share, 2 * share), 2 * share)]

    def solve(k):
        r = k // cycle
        value = out[r]
        low = (value - value.astype(jnp.bfloat16).astype(jnp.float32)).astype(jnp.bfloat16)
        none = jnp.zeros_like(low)
        first = core == 0
        low = jnp.concatenate([jnp.where(first, low, none), jnp.where(first, none, low)], axis=0)
        start = pair_dot(k, chip, low)
        earlier(lambda other: (arrived(gathered, g_recv, k, other * 2 + core),
                               g_pass(k, other).start()) and None)
        arrived(gathered, g_recv, k, partner)
        out[r] = start + pair_dot(k, chip, pair(k, chip))

        def add(other):
            arrived(gathered, g_recv, k, other * 2 + 1 - core)
            out[r] += pair_dot(k, other, pair(k, other))

        earlier(add)
        solved[k, mine] = out[r].astype(jnp.bfloat16)
        for d in range(1, cycle):
            b_out(k, d).start()

    def update(k, r):
        @pl.when(r * cycle + position > k)
        def _():
            out[r] -= jnp.dot(held[r, k], solved[k], preferred_element_type=jnp.float32)

    out[...] = loads[...]
    pl.semaphore_wait(barrier, 1 + (chips - 1) + (cycle - 1))

    pl.when(position == 0)(lambda: gather_work(0))
    for k in range(steps):
        owner = k % cycle
        for r in range(rounds):
            fetch(r, k).wait()
        pl.when(position == owner)(lambda: solve(k))
        pl.when(position != owner)(lambda: arrived(solved, s_recv, k, place))
        others(far, lambda other: s_out(k, other).start())
        s_pass(k, chip).start()
        others(near, lambda other: (arrived(solved, s_recv, k, other * 2 + core),
                                    s_pass(k, other).start()) and None)
        arrived(solved, s_recv, k, partner)
        others(near, lambda other: arrived(solved, s_recv, k, other * 2 + 1 - core))
        first = (k + 1) // cycle if k + 1 < steps else 0
        update(k, first)
        if k + 1 < steps:
            pl.when(position == (k + 1) % cycle)(lambda: gather_work(k + 1))
        for r in range(rounds):
            if r != first:
                update(k, r)

    for k in range(steps):
        @pl.when(position == k % cycle)
        def _():
            later(lambda other: g_out(k, other).wait_send())
            earlier(lambda other: g_pass(k, other).wait_send())
            g_pass(k, chip).wait_send()
            for d in range(1, cycle):
                b_out(k, d).wait_send()
        others(far, lambda other: s_out(k, other).wait_send())
        others(far, lambda other: s_pass(k, other).wait_send())
        s_pass(k, chip).wait_send()


def body(factor, loads):
    cycle = lax.axis_size("blk")
    places = lax.axis_size("rhs")
    rounds, _, share, width = factor.shape
    cases = loads.shape[3]
    block = share * places
    steps = width // block
    chips = places // 2
    dma = pltpu.SemaphoreType.DMA
    result = pl.pallas_call(
        functools.partial(kernel, (cycle, places, steps, rounds, share, block, cases)),
        out_shape=jax.ShapeDtypeStruct((rounds, share, cases), jnp.float32),
        in_specs=[pl.BlockSpec(memory_space=pl.ANY), pl.BlockSpec(memory_space=pltpu.VMEM)],
        out_specs=pl.BlockSpec(memory_space=pltpu.VMEM),
        scratch_shapes=[
            pltpu.VMEM((rounds, steps, share, block), jnp.bfloat16),
            pltpu.VMEM((steps, block, cases), jnp.bfloat16),
            pltpu.VMEM((steps, block, cases), jnp.bfloat16),
            dma((rounds, steps)),
            dma((steps, places)),
            dma((steps, places)),
            dma((steps, chips)),
            dma((steps, chips)),
            dma((steps, cycle)),
            dma((steps, chips)),
            dma((steps, chips)),
        ],
        compiler_params=pltpu.CompilerParams(
            collective_id=0, has_side_effects=True, vmem_limit_bytes=40 * 2**20),
    )(factor[:, 0], loads[:, 0])
    return result[:, None]


def solution(mesh):
    return jax.shard_map(
        body,
        mesh=mesh,
        in_specs=(P(None, "blk", "rhs", None), P(None, "blk", "rhs", None)),
        out_specs=P(None, "blk", "rhs", None),
        check_vma=False,
    )
```

```python
import functools

import jax
import jax.numpy as jnp
from jax import lax
from jax.experimental import pallas as pl
from jax.experimental.pallas import tpu as pltpu
from jax.sharding import PartitionSpec as P

MESH = pl.DeviceIdType.MESH


def kernel(dims, factor, loads, out, held, gathered, solved, total, load_sem, loads_sem, g_recv,
           s_recv, g_send, gp_send, b_send, s_send, sp_send):
    cycle, places, steps, rounds, share, block, cases = dims
    chips = places // 2
    half = share // 2
    position = lax.axis_index("blk")
    place = lax.axis_index("rhs")
    chip = place // 2
    core = place % 2
    partner = place + 1 - 2 * core

    def fetch(r, k):
        return pltpu.make_async_copy(
            factor.at[r, :, pl.ds(k * block, block)], held.at[r, k], load_sem.at[r, k])

    for k in range(steps):
        for r in range(rounds):
            fetch(r, k).start()

    barrier = pltpu.get_barrier_semaphore()
    pl.semaphore_signal(barrier, inc=1, device_id={"rhs": partner}, device_id_type=MESH)
    for d in range(1, chips):
        pl.semaphore_signal(barrier, inc=1, device_id={"rhs": (chip + d) % chips * 2 + core},
                            device_id_type=MESH)
    for d in range(1, cycle):
        pl.semaphore_signal(barrier, inc=1, device_id={"blk": (position + d) % cycle},
                            device_id_type=MESH)

    def copy(buffer, recv, k, h, source, send, device):
        rows = pl.ds(pl.multiple_of(source * half, half), half)
        return pltpu.make_async_remote_copy(
            src_ref=buffer.at[k, h, rows], dst_ref=buffer.at[k, h, rows], send_sem=send,
            recv_sem=recv.at[k, h, source], device_id=device, device_id_type=MESH)

    def arrived(buffer, recv, k, h, source):
        copy(buffer, recv, k, h, source, s_send.at[k, h, 0], {"rhs": partner}).wait_recv()

    def others(order, body):
        for d in order:
            for sign in (1, -1):
                other = chip + sign * d
                pl.when((other >= 0) & (other < chips))(functools.partial(body, other))

    near = range(1, chips)
    far = range(chips - 1, 0, -1)

    def later(body):
        for d in far:
            other = chip + d
            pl.when(other < chips)(functools.partial(body, other))

    def earlier(body):
        for d in near:
            other = chip - d
            pl.when(other >= 0)(functools.partial(body, other))

    def g_out(k, h, other):
        return copy(gathered, g_recv, k, h, place, g_send.at[k, h, other],
                    {"rhs": other * 2 + core})

    def g_pass(k, h, other):
        return copy(gathered, g_recv, k, h, other * 2 + core, gp_send.at[k, h, other],
                    {"rhs": partner})

    def s_out(k, h, other):
        return copy(solved, s_recv, k, h, place, s_send.at[k, h, other],
                    {"rhs": other * 2 + core})

    def s_pass(k, h, other):
        return copy(solved, s_recv, k, h, other * 2 + core, sp_send.at[k, h, other],
                    {"rhs": partner})

    def b_out(k, h, d):
        return copy(solved, s_recv, k, h, place, b_send.at[k, h, d],
                    {"blk": (k % cycle + d) % cycle})

    mine = pl.ds(pl.multiple_of(place * half, half), half)
    lanes = cases // 2

    def own_lanes(h, rows):
        low = lax.broadcasted_iota(jnp.int32, (rows, cases), 1) < lanes
        return low if h == 0 else jnp.logical_not(low)

    def pack(h, value):
        turned = pltpu.roll(value[half:], lanes, 1)
        return jnp.where(own_lanes(h, half), value[:half], turned).astype(jnp.bfloat16)

    def unpack(packed):
        count = packed.shape[0] // half
        turned = pltpu.roll(packed.astype(jnp.float32), lanes, 1).astype(jnp.bfloat16)
        both = jnp.concatenate(
            [packed.reshape(count, half, cases), turned.reshape(count, half, cases)], axis=1)
        return both.reshape(count * share, cases)

    def gather_work(k, h):
        gathered[k, h, mine] = pack(h, out[k // cycle])
        later(lambda other: g_out(k, h, other).start())
        g_pass(k, h, chip).start()

    def pair_dot(k, other, value):
        columns = pl.ds(pl.multiple_of(other * 2 * share, 2 * share), 2 * share)
        return jnp.dot(held[k // cycle, k, :, columns], value, preferred_element_type=jnp.float32)

    def pair(k, h, other):
        return unpack(gathered[k, h, pl.ds(pl.multiple_of(other * share, share), share)])

    def solve(k, h):
        r = k // cycle
        value = out[r]
        low = (value - value.astype(jnp.bfloat16).astype(jnp.float32)).astype(jnp.bfloat16)
        none = jnp.zeros_like(low)
        first = core == 0
        low = jnp.concatenate([jnp.where(first, low, none), jnp.where(first, none, low)], axis=0)
        total[...] = pair_dot(k, chip, low)
        earlier(lambda other: (arrived(gathered, g_recv, k, h, other * 2 + core),
                               g_pass(k, h, other).start()) and None)
        arrived(gathered, g_recv, k, h, partner)
        total[...] += pair_dot(k, chip, pair(k, h, chip))

        def add(other):
            arrived(gathered, g_recv, k, h, other * 2 + 1 - core)
            total[...] += pair_dot(k, other, pair(k, h, other))

        earlier(add)
        result = total[...]
        solved[k, h, mine] = pack(h, result)
        for d in range(1, cycle):
            b_out(k, h, d).start()
        out[r] = jnp.where(own_lanes(h, share), result, out[r])

    def update(k, h, r):
        @pl.when(r * cycle + position > k)
        def _():
            change = jnp.dot(held[r, k], unpack(solved[k, h]), preferred_element_type=jnp.float32)
            out[r] = jnp.where(own_lanes(h, share), out[r] - change, out[r])

    pltpu.make_async_copy(loads, out, loads_sem).start()
    pltpu.make_async_copy(loads, out, loads_sem).wait()
    pl.semaphore_wait(barrier, 1 + (chips - 1) + (cycle - 1))

    @pl.when(position == 0)
    def _():
        for h in range(2):
            gather_work(0, h)

    waiting = []
    for k in range(steps):
        owner = k % cycle
        for r in range(rounds):
            fetch(r, k).wait()
        for h in range(2):
            pl.when(position == owner)(lambda: solve(k, h))
            pl.when(position != owner)(lambda: arrived(solved, s_recv, k, h, place))
            others(far, lambda other: s_out(k, h, other).start())
            s_pass(k, h, chip).start()
        for each in waiting:
            update(*each)
        waiting = []
        first = (k + 1) // cycle if k + 1 < steps else 0
        for h in range(2):
            others(near, lambda other: (arrived(solved, s_recv, k, h, other * 2 + core),
                                        s_pass(k, h, other).start()) and None)
            arrived(solved, s_recv, k, h, partner)
            others(near, lambda other: arrived(solved, s_recv, k, h, other * 2 + 1 - core))
            update(k, h, first)
            if k + 1 < steps:
                pl.when(position == (k + 1) % cycle)(lambda: gather_work(k + 1, h))
            waiting += [(k, h, r) for r in range(rounds) if r != first]
    for each in waiting:
        update(*each)

    for k in range(steps):
        for h in range(2):
            @pl.when(position == k % cycle)
            def _():
                later(lambda other: g_out(k, h, other).wait_send())
                earlier(lambda other: g_pass(k, h, other).wait_send())
                g_pass(k, h, chip).wait_send()
                for d in range(1, cycle):
                    b_out(k, h, d).wait_send()
            others(far, lambda other: s_out(k, h, other).wait_send())
            others(far, lambda other: s_pass(k, h, other).wait_send())
            s_pass(k, h, chip).wait_send()


def body(factor, loads):
    cycle = lax.axis_size("blk")
    places = lax.axis_size("rhs")
    rounds, _, share, width = factor.shape
    cases = loads.shape[3]
    block = share * places
    steps = width // block
    chips = places // 2
    dma = pltpu.SemaphoreType.DMA
    result = pl.pallas_call(
        functools.partial(kernel, (cycle, places, steps, rounds, share, block, cases)),
        out_shape=jax.ShapeDtypeStruct((rounds, share, cases), jnp.float32),
        in_specs=[pl.BlockSpec(memory_space=pl.ANY)] * 2,
        out_specs=pl.BlockSpec(memory_space=pltpu.VMEM),
        scratch_shapes=[
            pltpu.VMEM((rounds, steps, share, block), jnp.bfloat16),
            pltpu.VMEM((steps, 2, block // 2, cases), jnp.bfloat16),
            pltpu.VMEM((steps, 2, block // 2, cases), jnp.bfloat16),
            pltpu.VMEM((share, cases), jnp.float32),
            dma((rounds, steps)),
            dma,
            dma((steps, 2, places)),
            dma((steps, 2, places)),
            dma((steps, 2, chips)),
            dma((steps, 2, chips)),
            dma((steps, 2, cycle)),
            dma((steps, 2, chips)),
            dma((steps, 2, chips)),
        ],
        compiler_params=pltpu.CompilerParams(
            collective_id=0, has_side_effects=True, vmem_limit_bytes=60 * 2**20),
    )(factor[:, 0], loads[:, 0])
    return result[:, None]


def solution(mesh):
    return jax.shard_map(
        body,
        mesh=mesh,
        in_specs=(P(None, "blk", "rhs", None), P(None, "blk", "rhs", None)),
        out_specs=P(None, "blk", "rhs", None),
        check_vma=False,
    )
```

```python
import functools

import jax
import jax.numpy as jnp
from jax import lax
from jax.experimental import pallas as pl
from jax.experimental.pallas import tpu as pltpu
from jax.sharding import PartitionSpec as P

MESH = pl.DeviceIdType.MESH


def kernel(dims, factor, loads, out, held, gathered, solved, total, load_sem, loads_sem, g_recv,
           s_recv, g_send, gp_send, b_send, s_send, sp_send, c_send):
    cycle, places, steps, rounds, share, block, cases = dims
    chips = places // 2
    half = share // 2
    position = lax.axis_index("blk")
    place = lax.axis_index("rhs")
    chip = place // 2
    core = place % 2
    partner = place + 1 - 2 * core

    def fetch(r, k):
        return pltpu.make_async_copy(
            factor.at[r, :, pl.ds(k * block, block)], held.at[r, k], load_sem.at[r, k])

    for k in range(steps):
        for r in range(rounds):
            fetch(r, k).start()

    barrier = pltpu.get_barrier_semaphore()
    pl.semaphore_signal(barrier, inc=1, device_id={"rhs": partner}, device_id_type=MESH)
    for d in range(1, chips):
        pl.semaphore_signal(barrier, inc=1, device_id={"rhs": (chip + d) % chips * 2 + core},
                            device_id_type=MESH)
    for d in range(1, cycle):
        pl.semaphore_signal(barrier, inc=1, device_id={"blk": (position + d) % cycle},
                            device_id_type=MESH)

    for step in {1, cycle - 1}:
        for d in range(1, chips):
            pl.semaphore_signal(
                barrier, inc=1, device_id_type=MESH,
                device_id={"blk": (position + step) % cycle,
                           "rhs": (chip + d) % chips * 2 + core})

    def copy(buffer, recv, k, h, source, send, device):
        rows = pl.ds(pl.multiple_of(source * half, half), half)
        return pltpu.make_async_remote_copy(
            src_ref=buffer.at[k, h, rows], dst_ref=buffer.at[k, h, rows], send_sem=send,
            recv_sem=recv.at[k, h, source], device_id=device, device_id_type=MESH)

    def arrived(buffer, recv, k, h, source):
        copy(buffer, recv, k, h, source, s_send.at[k, h, 0], {"rhs": partner}).wait_recv()

    def others(order, body):
        for d in order:
            for sign in (1, -1):
                other = chip + sign * d
                pl.when((other >= 0) & (other < chips))(functools.partial(body, other))

    near = range(1, chips)
    far = range(chips - 1, 0, -1)

    def later(body):
        for d in far:
            other = chip + d
            pl.when(other < chips)(functools.partial(body, other))

    def earlier(body):
        for d in near:
            other = chip - d
            pl.when(other >= 0)(functools.partial(body, other))

    def g_out(k, h, other):
        return copy(gathered, g_recv, k, h, place, g_send.at[k, h, other],
                    {"rhs": other * 2 + core})

    def g_pass(k, h, other):
        return copy(gathered, g_recv, k, h, other * 2 + core, gp_send.at[k, h, other],
                    {"rhs": partner})

    def s_out(k, h, other):
        return copy(solved, s_recv, k, h, place, s_send.at[k, h, other],
                    {"rhs": other * 2 + core})

    def s_pass(k, h, other):
        return copy(solved, s_recv, k, h, other * 2 + core, sp_send.at[k, h, other],
                    {"rhs": partner})

    def b_out(k, h, d):
        return copy(solved, s_recv, k, h, place, b_send.at[k, h, d],
                    {"blk": (k % cycle + d) % cycle})

    def c_out(k, h, other):
        return copy(solved, s_recv, k, h, place, c_send.at[k, h, other],
                    {"blk": (k + 1) % cycle, "rhs": other * 2 + core})

    mine = pl.ds(pl.multiple_of(place * half, half), half)
    lanes = cases // 2

    def own_lanes(h, rows):
        low = lax.broadcasted_iota(jnp.int32, (rows, cases), 1) < lanes
        return low if h == 0 else jnp.logical_not(low)

    def pack(h, value):
        turned = pltpu.roll(value[half:], lanes, 1)
        return jnp.where(own_lanes(h, half), value[:half], turned).astype(jnp.bfloat16)

    def unpack(packed):
        count = packed.shape[0] // half
        turned = pltpu.roll(packed.astype(jnp.float32), lanes, 1).astype(jnp.bfloat16)
        both = jnp.concatenate(
            [packed.reshape(count, half, cases), turned.reshape(count, half, cases)], axis=1)
        return both.reshape(count * share, cases)

    def gather_work(k, h):
        gathered[k, h, mine] = pack(h, out[k // cycle])
        later(lambda other: g_out(k, h, other).start())
        g_pass(k, h, chip).start()

    def pair_dot(k, other, value, r=None):
        r = k // cycle if r is None else r
        columns = pl.ds(pl.multiple_of(other * 2 * share, 2 * share), 2 * share)
        return jnp.dot(held[r, k, :, columns], value, preferred_element_type=jnp.float32)

    def pair(buffer, k, h, other):
        return unpack(buffer[k, h, pl.ds(pl.multiple_of(other * share, share), share)])

    def stream(k, h, buffer, recv, forward, visit, ready, dot):
        if ready is not None:
            @pl.when(ready)
            def _():
                arrived(buffer, recv, k, h, place)
                forward(k, h, chip).start()

        def own(other):
            arrived(buffer, recv, k, h, other * 2 + core)
            forward(k, h, other).start()

        def pairs(other):
            arrived(buffer, recv, k, h, other * 2 + 1 - core)
            dot(other)

        if chips > 1:
            visit(1, own)
        pairs(chip)
        for d in range(1, chips):
            if d + 1 < chips:
                visit(d + 1, own)
            visit(d, pairs)

    def below(d, body):
        other = chip - d
        pl.when(other >= 0)(functools.partial(body, other))

    def around(d, body):
        others([d], body)

    def solve(k, h):
        r = k // cycle
        value = out[r]
        low = (value - value.astype(jnp.bfloat16).astype(jnp.float32)).astype(jnp.bfloat16)
        none = jnp.zeros_like(low)
        first = core == 0
        low = jnp.concatenate([jnp.where(first, low, none), jnp.where(first, none, low)], axis=0)
        total[...] = pair_dot(k, chip, low)

        def dot(other):
            total[...] += pair_dot(k, other, pair(gathered, k, h, other))

        stream(k, h, gathered, g_recv, g_pass, below, None, dot)
        solved[k, h, mine] = pack(h, total[...])
        if k + 1 < steps:
            for other in range(chips):
                c_out(k, h, other).start()
        s_pass(k, h, chip).start()
        out[r] = jnp.where(own_lanes(h, share), total[...], out[r])

    def receive(k, h, r):
        needed = r * cycle + position > k
        total[...] = jnp.zeros_like(total)

        def dot(other):
            @pl.when(needed)
            def _():
                total[...] += pair_dot(k, other, pair(solved, k, h, other), r)

        ready = position == (k + 1) % cycle if k + 1 < steps else None
        stream(k, h, solved, s_recv, s_pass, around, ready, dot)

        @pl.when(needed)
        def _():
            out[r] = jnp.where(own_lanes(h, share), out[r] - total[...], out[r])

    def update(k, h, r):
        @pl.when(r * cycle + position > k)
        def _():
            change = jnp.dot(held[r, k], unpack(solved[k, h]), preferred_element_type=jnp.float32)
            out[r] = jnp.where(own_lanes(h, share), out[r] - change, out[r])

    pltpu.make_async_copy(loads, out, loads_sem).start()
    pltpu.make_async_copy(loads, out, loads_sem).wait()
    pl.semaphore_wait(barrier, 1 + (cycle - 1) + 3 * (chips - 1))

    @pl.when(position == 0)
    def _():
        for h in range(2):
            gather_work(0, h)

    waiting = []
    for k in range(steps):
        owner = k % cycle
        for r in range(rounds):
            fetch(r, k).wait()
        nearby = 2 if k + 1 < steps else 1
        for h in range(2):
            pl.when(position == owner)(lambda: solve(k, h))

        def spread(h):
            @pl.when(position == owner)
            def _():
                for d in range(nearby, cycle):
                    b_out(k, h, d).start()

            @pl.when(position != owner)
            def _():
                arrived(solved, s_recv, k, h, place)
                s_pass(k, h, chip).start()

            others(far, lambda other: s_out(k, h, other).start())

        for h in range(2):
            if k + 1 < steps:
                pl.when(position != (k + 1) % cycle)(lambda: spread(h))
            else:
                spread(h)
        for each in waiting:
            update(*each)
        waiting = []
        first = (k + 1) // cycle if k + 1 < steps else rounds - 1
        for h in range(2):
            receive(k, h, first)
            if k + 1 < steps:
                pl.when(position == (k + 1) % cycle)(lambda: gather_work(k + 1, h))
            waiting += [(k, h, r) for r in range(rounds) if r != first]
    for each in waiting:
        update(*each)

    for k in range(steps):
        for h in range(2):
            @pl.when(position == k % cycle)
            def _():
                later(lambda other: g_out(k, h, other).wait_send())
                earlier(lambda other: g_pass(k, h, other).wait_send())
                g_pass(k, h, chip).wait_send()
                for d in range(2 if k + 1 < steps else 1, cycle):
                    b_out(k, h, d).wait_send()
                if k + 1 < steps:
                    for other in range(chips):
                        c_out(k, h, other).wait_send()

            sent = lambda: others(far, lambda other: s_out(k, h, other).wait_send())
            if k + 1 < steps:
                pl.when(position != (k + 1) % cycle)(sent)
            else:
                sent()
            others(far, lambda other: s_pass(k, h, other).wait_send())
            s_pass(k, h, chip).wait_send()


def body(factor, loads):
    cycle = lax.axis_size("blk")
    places = lax.axis_size("rhs")
    rounds, _, share, width = factor.shape
    cases = loads.shape[3]
    block = share * places
    steps = width // block
    chips = places // 2
    dma = pltpu.SemaphoreType.DMA
    result = pl.pallas_call(
        functools.partial(kernel, (cycle, places, steps, rounds, share, block, cases)),
        out_shape=jax.ShapeDtypeStruct((rounds, share, cases), jnp.float32),
        in_specs=[pl.BlockSpec(memory_space=pl.ANY)] * 2,
        out_specs=pl.BlockSpec(memory_space=pltpu.VMEM),
        scratch_shapes=[
            pltpu.VMEM((rounds, steps, share, block), jnp.bfloat16),
            pltpu.VMEM((steps, 2, block // 2, cases), jnp.bfloat16),
            pltpu.VMEM((steps, 2, block // 2, cases), jnp.bfloat16),
            pltpu.VMEM((share, cases), jnp.float32),
            dma((rounds, steps)),
            dma,
            dma((steps, 2, places)),
            dma((steps, 2, places)),
            dma((steps, 2, chips)),
            dma((steps, 2, chips)),
            dma((steps, 2, cycle)),
            dma((steps, 2, chips)),
            dma((steps, 2, chips)),
            dma((steps, 2, chips)),
        ],
        compiler_params=pltpu.CompilerParams(
            collective_id=0, has_side_effects=True, vmem_limit_bytes=60 * 2**20),
    )(factor[:, 0], loads[:, 0])
    return result[:, None]


def solution(mesh):
    return jax.shard_map(
        body,
        mesh=mesh,
        in_specs=(P(None, "blk", "rhs", None), P(None, "blk", "rhs", None)),
        out_specs=P(None, "blk", "rhs", None),
        check_vma=False,
    )
```

```python
import functools

import jax
import jax.numpy as jnp
from jax import lax
from jax.experimental import pallas as pl
from jax.experimental.pallas import tpu as pltpu
from jax.sharding import PartitionSpec as P

MESH = pl.DeviceIdType.MESH


def kernel(dims, factor, loads, out, held, gathered, solved, total, load_sem, loads_sem, g_recv,
           s_recv, g_send, gp_send, b_send, s_send, sp_send, c_send):
    cycle, places, steps, rounds, share, block, cases = dims
    chips = places // 2
    half = share // 2
    position = lax.axis_index("blk")
    place = lax.axis_index("rhs")
    chip = place // 2
    core = place % 2
    partner = place + 1 - 2 * core

    def fetch(r, k):
        return pltpu.make_async_copy(
            factor.at[r, :, pl.ds(k * block, block)], held.at[r, k], load_sem.at[r, k])

    for k in range(steps):
        for r in range(rounds):
            fetch(r, k).start()

    barrier = pltpu.get_barrier_semaphore()
    pl.semaphore_signal(barrier, inc=1, device_id={"rhs": partner}, device_id_type=MESH)
    for d in range(1, chips):
        pl.semaphore_signal(barrier, inc=1, device_id={"rhs": (chip + d) % chips * 2 + core},
                            device_id_type=MESH)
    for d in range(1, cycle):
        pl.semaphore_signal(barrier, inc=1, device_id={"blk": (position + d) % cycle},
                            device_id_type=MESH)

    def copy(buffer, recv, k, h, source, send, device):
        rows = pl.ds(pl.multiple_of(source * half, half), half)
        return pltpu.make_async_remote_copy(
            src_ref=buffer.at[k, h, rows], dst_ref=buffer.at[k, h, rows], send_sem=send,
            recv_sem=recv.at[k, h, source], device_id=device, device_id_type=MESH)

    def arrived(buffer, recv, k, h, source):
        copy(buffer, recv, k, h, source, s_send.at[k, h, chips], {"rhs": partner}).wait_recv()

    started = []

    def begin(where, what):
        started.append((where, what))
        pl.when(where())(lambda: what().start())

    def inside(other):
        return (other >= 0) & (other < chips)

    def g_out(k, h, d):
        begin(lambda: (position == k % cycle) & inside(chip + d),
              lambda: copy(gathered, g_recv, k, h, place, g_send.at[k, h, d],
                           {"rhs": (chip + d) * 2 + core}))

    def g_forward(k, h, d):
        begin(lambda: (position == k % cycle) & inside(chip - d) & inside(chip + 1),
              lambda: copy(gathered, g_recv, k, h, (chip - d) * 2 + core, g_send.at[k, h, 1 + d],
                           {"rhs": (chip + 1) * 2 + core}))

    def g_pass(k, h, d):
        begin(lambda: (position == k % cycle) & inside(chip - d),
              lambda: copy(gathered, g_recv, k, h, (chip - d) * 2 + core, gp_send.at[k, h, d],
                           {"rhs": partner}))

    def direct(k, h):
        return k + 1 < steps and h == 1

    def goes(k, h):
        return position != (k + 1) % cycle if direct(k, h) else position >= 0

    def s_out(k, h, d):
        begin(lambda: goes(k, h) & inside(chip + d),
              lambda: copy(solved, s_recv, k, h, place, s_send.at[k, h, d + chips],
                           {"rhs": (chip + d) * 2 + core}))

    def anyone():
        return position >= 0

    def s_forward(k, h, d, who):
        sign = 1 if d > 0 else -1
        slot = sign * (abs(d) + 1) + chips
        begin(lambda: who() & goes(k, h) & inside(chip + d) & inside(chip - sign),
              lambda: copy(solved, s_recv, k, h, (chip + d) * 2 + core, s_send.at[k, h, slot],
                           {"rhs": (chip - sign) * 2 + core}))

    def s_pass(k, h, d, who=anyone):
        begin(lambda: who() & inside(chip + d),
              lambda: copy(solved, s_recv, k, h, (chip + d) * 2 + core,
                           sp_send.at[k, h, d + chips], {"rhs": partner}))

    def b_out(k, h, d):
        begin(lambda: position == k % cycle,
              lambda: copy(solved, s_recv, k, h, place, b_send.at[k, h, d],
                           {"blk": (k % cycle + d) % cycle}))

    def cross(k, h, d):
        begin(lambda: (position == k % cycle) & inside(chip + d),
              lambda: copy(solved, s_recv, k, h, (chip + d) * 2 + core, c_send.at[k, h, d + chips],
                           {"blk": (k + 1) % cycle}))

    mine = pl.ds(pl.multiple_of(place * half, half), half)
    lanes = cases // 2

    def own_lanes(h, rows):
        low = lax.broadcasted_iota(jnp.int32, (rows, cases), 1) < lanes
        return low if h == 0 else jnp.logical_not(low)

    def pack(h, value):
        turned = pltpu.roll(value[half:], lanes, 1)
        return jnp.where(own_lanes(h, half), value[:half], turned).astype(jnp.bfloat16)

    def unpack(packed):
        count = packed.shape[0] // half
        turned = pltpu.roll(packed.astype(jnp.float32), lanes, 1).astype(jnp.bfloat16)
        both = jnp.concatenate(
            [packed.reshape(count, half, cases), turned.reshape(count, half, cases)], axis=1)
        return both.reshape(count * share, cases)

    def gather_work(k, h):
        @pl.when(position == k % cycle)
        def _():
            gathered[k, h, mine] = pack(h, out[k // cycle])

        for d in (2, 1):
            if d < chips:
                g_out(k, h, d)
        g_pass(k, h, 0)

    def pair_dot(k, other, value):
        columns = pl.ds(pl.multiple_of(other * 2 * share, 2 * share), 2 * share)
        return jnp.dot(held[k // cycle, k, :, columns], value, preferred_element_type=jnp.float32)

    def pair(k, h, other):
        return unpack(gathered[k, h, pl.ds(pl.multiple_of(other * share, share), share)])

    def solve(k, h):
        r = k // cycle
        value = out[r]
        low = (value - value.astype(jnp.bfloat16).astype(jnp.float32)).astype(jnp.bfloat16)
        none = jnp.zeros_like(low)
        first = core == 0
        low = jnp.concatenate([jnp.where(first, low, none), jnp.where(first, none, low)], axis=0)
        total[...] = pair_dot(k, chip, low)
        for d in range(1, chips):
            pl.when(chip >= d)(lambda: arrived(gathered, g_recv, k, h, (chip - d) * 2 + core))
            if d >= 2:
                g_forward(k, h, d)
            g_pass(k, h, d)
        arrived(gathered, g_recv, k, h, partner)
        total[...] += pair_dot(k, chip, pair(k, h, chip))

        def add(other):
            arrived(gathered, g_recv, k, h, other * 2 + 1 - core)
            total[...] += pair_dot(k, other, pair(k, h, other))

        for d in range(1, chips):
            pl.when(chip >= d)(lambda: add(chip - d))
        result = total[...]
        solved[k, h, mine] = pack(h, result)
        out[r] = jnp.where(own_lanes(h, share), result, out[r])

    def update(k, h, r):
        @pl.when(r * cycle + position > k)
        def _():
            change = jnp.dot(held[r, k], unpack(solved[k, h]), preferred_element_type=jnp.float32)
            out[r] = jnp.where(own_lanes(h, share), out[r] - change, out[r])

    pltpu.make_async_copy(loads, out, loads_sem).start()
    pltpu.make_async_copy(loads, out, loads_sem).wait()
    pl.semaphore_wait(barrier, 1 + (chips - 1) + (cycle - 1))

    def near():
        return [sign * d for d in range(1, chips) for sign in (1, -1)]

    def relay(k, h, who, first=False):
        for d in near():
            pl.when(who() & inside(chip + d))(
                lambda: arrived(solved, s_recv, k, h, (chip + d) * 2 + core))
            if direct(k, h) and first:
                cross(k, h, d)
            if abs(d) >= 2:
                s_forward(k, h, d, who)
            s_pass(k, h, d, who)
        pl.when(who())(lambda: arrived(solved, s_recv, k, h, partner))
        for d in near():
            pl.when(who() & inside(chip + d))(
                lambda: arrived(solved, s_recv, k, h, (chip + d) * 2 + 1 - core))

    for h in range(2):
        gather_work(0, h)

    waiting = []
    for k in range(steps):
        owner = k % cycle
        final = k + 1 == steps
        for r in range(rounds):
            fetch(r, k).wait()

        for h in range(2):
            pl.when(position == owner)(lambda: solve(k, h))
            pl.when(position != owner)(lambda: arrived(solved, s_recv, k, h, place))
            if direct(k, h):
                cross(k, h, 0)
            else:
                b_out(k, h, 1)
            if final:
                for d in range(2, cycle):
                    b_out(k, h, d)
            for d in (2, -2, 1, -1):
                if abs(d) < chips:
                    s_out(k, h, d)
            s_pass(k, h, 0)
        if not final:
            for h in range(2):
                for d in range(2, cycle):
                    b_out(k, h, d)
        for each in waiting:
            update(*each)
        waiting = []
        first = (k + 1) // cycle if not final else 0
        if not final:
            relay(k, 1, lambda owner=owner: position == owner, True)
        for h in range(2):
            if direct(k, h):
                relay(k, h, lambda owner=owner: position != owner)
            else:
                relay(k, h, anyone)
            update(k, h, first)
            if not final:
                gather_work(k + 1, h)
            waiting += [(k, h, r) for r in range(rounds) if r != first]
    for each in waiting:
        update(*each)
    for where, what in started:
        pl.when(where())(lambda: what().wait_send())


def body(factor, loads):
    cycle = lax.axis_size("blk")
    places = lax.axis_size("rhs")
    rounds, _, share, width = factor.shape
    cases = loads.shape[3]
    block = share * places
    steps = width // block
    chips = places // 2
    dma = pltpu.SemaphoreType.DMA
    result = pl.pallas_call(
        functools.partial(kernel, (cycle, places, steps, rounds, share, block, cases)),
        out_shape=jax.ShapeDtypeStruct((rounds, share, cases), jnp.float32),
        in_specs=[pl.BlockSpec(memory_space=pl.ANY)] * 2,
        out_specs=pl.BlockSpec(memory_space=pltpu.VMEM),
        scratch_shapes=[
            pltpu.VMEM((rounds, steps, share, block), jnp.bfloat16),
            pltpu.VMEM((steps, 2, block // 2, cases), jnp.bfloat16),
            pltpu.VMEM((steps, 2, block // 2, cases), jnp.bfloat16),
            pltpu.VMEM((share, cases), jnp.float32),
            dma((rounds, steps)),
            dma,
            dma((steps, 2, places)),
            dma((steps, 2, places)),
            dma((steps, 2, chips + 1)),
            dma((steps, 2, chips)),
            dma((steps, 2, cycle)),
            dma((steps, 2, 2 * chips + 1)),
            dma((steps, 2, 2 * chips)),
            dma((steps, 2, 2 * chips)),
        ],
        compiler_params=pltpu.CompilerParams(
            collective_id=0, has_side_effects=True, vmem_limit_bytes=60 * 2**20),
    )(factor[:, 0], loads[:, 0])
    return result[:, None]


def solution(mesh):
    return jax.shard_map(
        body,
        mesh=mesh,
        in_specs=(P(None, "blk", "rhs", None), P(None, "blk", "rhs", None)),
        out_specs=P(None, "blk", "rhs", None),
        check_vma=False,
    )
```

```python
import functools

import jax
import jax.numpy as jnp
from jax import lax
from jax.experimental import pallas as pl
from jax.experimental.pallas import tpu as pltpu
from jax.sharding import PartitionSpec as P

MESH = pl.DeviceIdType.MESH


def kernel(dims, factor, loads, out, held, gathered, solved, total, load_sem, loads_sem, g_recv,
           s_recv, g_send, gp_send, b_send, s_send, sp_send, c_send):
    cycle, places, steps, rounds, share, block, cases = dims
    chips = places // 2
    half = share // 2
    position = lax.axis_index("blk")
    place = lax.axis_index("rhs")
    chip = place // 2
    core = place % 2
    partner = place + 1 - 2 * core

    def fetch(r, k):
        return pltpu.make_async_copy(
            factor.at[r, :, pl.ds(k * block, block)], held.at[r, k], load_sem.at[r, k])

    for k in range(steps):
        for r in range(rounds):
            fetch(r, k).start()

    barrier = pltpu.get_barrier_semaphore()
    pl.semaphore_signal(barrier, inc=1, device_id={"rhs": partner}, device_id_type=MESH)
    for d in range(1, chips):
        pl.semaphore_signal(barrier, inc=1, device_id={"rhs": (chip + d) % chips * 2 + core},
                            device_id_type=MESH)
    for d in range(1, cycle):
        pl.semaphore_signal(barrier, inc=1, device_id={"blk": (position + d) % cycle},
                            device_id_type=MESH)

    for step in {1, cycle - 1}:
        for d in range(1, chips):
            pl.semaphore_signal(
                barrier, inc=1, device_id_type=MESH,
                device_id={"blk": (position + step) % cycle,
                           "rhs": (chip + d) % chips * 2 + core})

    def copy(buffer, recv, k, h, source, send, device):
        rows = pl.ds(pl.multiple_of(source * half, half), half)
        return pltpu.make_async_remote_copy(
            src_ref=buffer.at[k, h, rows], dst_ref=buffer.at[k, h, rows], send_sem=send,
            recv_sem=recv.at[k, h, source], device_id=device, device_id_type=MESH)

    def arrived(buffer, recv, k, h, source):
        copy(buffer, recv, k, h, source, s_send.at[k, h, 0], {"rhs": partner}).wait_recv()

    def others(order, body):
        for d in order:
            for sign in (1, -1):
                other = chip + sign * d
                pl.when((other >= 0) & (other < chips))(functools.partial(body, other))

    near = range(1, chips)
    far = range(chips - 1, 0, -1)

    def later(body):
        for d in far:
            other = chip + d
            pl.when(other < chips)(functools.partial(body, other))

    def earlier(body):
        for d in near:
            other = chip - d
            pl.when(other >= 0)(functools.partial(body, other))

    def g_out(k, h, other):
        return copy(gathered, g_recv, k, h, place, g_send.at[k, h, other],
                    {"rhs": other * 2 + core})

    def g_pass(k, h, other):
        return copy(gathered, g_recv, k, h, other * 2 + core, gp_send.at[k, h, other],
                    {"rhs": partner})

    def s_out(k, h, other):
        return copy(solved, s_recv, k, h, place, s_send.at[k, h, other],
                    {"rhs": other * 2 + core})

    def s_pass(k, h, other):
        return copy(solved, s_recv, k, h, other * 2 + core, sp_send.at[k, h, other],
                    {"rhs": partner})

    def b_out(k, h, d):
        return copy(solved, s_recv, k, h, place, b_send.at[k, h, d],
                    {"blk": (k % cycle + d) % cycle})

    def c_out(k, h, other):
        return copy(solved, s_recv, k, h, place, c_send.at[k, h, other],
                    {"blk": (k + 1) % cycle, "rhs": other * 2 + core})

    mine = pl.ds(pl.multiple_of(place * half, half), half)
    lanes = cases // 2

    def own_lanes(h, rows):
        low = lax.broadcasted_iota(jnp.int32, (rows, cases), 1) < lanes
        return low if h == 0 else jnp.logical_not(low)

    def pack(h, value):
        turned = pltpu.roll(value[half:], lanes, 1)
        return jnp.where(own_lanes(h, half), value[:half], turned).astype(jnp.bfloat16)

    def unpack(packed):
        count = packed.shape[0] // half
        turned = pltpu.roll(packed.astype(jnp.float32), lanes, 1).astype(jnp.bfloat16)
        both = jnp.concatenate(
            [packed.reshape(count, half, cases), turned.reshape(count, half, cases)], axis=1)
        return both.reshape(count * share, cases)

    def gather_work(k, h):
        gathered[k, h, mine] = pack(h, out[k // cycle])
        later(lambda other: g_out(k, h, other).start())
        g_pass(k, h, chip).start()

    def pair_dot(k, other, value, r=None):
        r = k // cycle if r is None else r
        columns = pl.ds(pl.multiple_of(other * 2 * share, 2 * share), 2 * share)
        return jnp.dot(held[r, k, :, columns], value, preferred_element_type=jnp.float32)

    def pair(buffer, k, h, other):
        return unpack(buffer[k, h, pl.ds(pl.multiple_of(other * share, share), share)])

    def solve(k, h):
        r = k // cycle
        value = out[r]
        low = (value - value.astype(jnp.bfloat16).astype(jnp.float32)).astype(jnp.bfloat16)
        none = jnp.zeros_like(low)
        first = core == 0
        low = jnp.concatenate([jnp.where(first, low, none), jnp.where(first, none, low)], axis=0)
        total[...] = pair_dot(k, chip, low)

        earlier(lambda other: (arrived(gathered, g_recv, k, h, other * 2 + core),
                               g_pass(k, h, other).start()) and None)
        arrived(gathered, g_recv, k, h, partner)
        total[...] += pair_dot(k, chip, pair(gathered, k, h, chip))

        def add(other):
            arrived(gathered, g_recv, k, h, other * 2 + 1 - core)
            total[...] += pair_dot(k, other, pair(gathered, k, h, other))

        earlier(add)
        solved[k, h, mine] = pack(h, total[...])
        if k + 1 < steps:
            for other in range(chips):
                c_out(k, h, other).start()
        s_pass(k, h, chip).start()
        out[r] = jnp.where(own_lanes(h, share), total[...], out[r])

    def receive(k, h):
        if k + 1 < steps:
            @pl.when(position == (k + 1) % cycle)
            def _():
                arrived(solved, s_recv, k, h, place)
                s_pass(k, h, chip).start()
        others(near, lambda other: (arrived(solved, s_recv, k, h, other * 2 + core),
                                    s_pass(k, h, other).start()) and None)
        arrived(solved, s_recv, k, h, partner)
        others(near, lambda other: arrived(solved, s_recv, k, h, other * 2 + 1 - core))

    def update(k, h, r):
        @pl.when(r * cycle + position > k)
        def _():
            change = jnp.dot(held[r, k], unpack(solved[k, h]), preferred_element_type=jnp.float32)
            out[r] = jnp.where(own_lanes(h, share), out[r] - change, out[r])

    pltpu.make_async_copy(loads, out, loads_sem).start()
    pltpu.make_async_copy(loads, out, loads_sem).wait()
    pl.semaphore_wait(barrier, 1 + (cycle - 1) + 3 * (chips - 1))

    @pl.when(position == 0)
    def _():
        for h in range(2):
            gather_work(0, h)

    waiting = []
    for k in range(steps):
        owner = k % cycle
        for r in range(rounds):
            fetch(r, k).wait()
        nearby = 2 if k + 1 < steps else 1
        for h in range(2):
            pl.when(position == owner)(lambda: solve(k, h))

        def spread(h):
            @pl.when(position == owner)
            def _():
                for d in range(nearby, cycle):
                    b_out(k, h, d).start()

            @pl.when(position != owner)
            def _():
                arrived(solved, s_recv, k, h, place)
                s_pass(k, h, chip).start()

            others(far, lambda other: s_out(k, h, other).start())

        for h in range(2):
            if k + 1 < steps:
                pl.when(position != (k + 1) % cycle)(lambda: spread(h))
            else:
                spread(h)
        for each in waiting:
            update(*each)
        waiting = []
        first = (k + 1) // cycle if k + 1 < steps else rounds - 1
        for h in range(2):
            receive(k, h)
            update(k, h, first)
            if k + 1 < steps:
                pl.when(position == (k + 1) % cycle)(lambda: gather_work(k + 1, h))
            waiting += [(k, h, r) for r in range(rounds) if r != first]
    for each in waiting:
        update(*each)

    for k in range(steps):
        for h in range(2):
            @pl.when(position == k % cycle)
            def _():
                later(lambda other: g_out(k, h, other).wait_send())
                earlier(lambda other: g_pass(k, h, other).wait_send())
                g_pass(k, h, chip).wait_send()
                for d in range(2 if k + 1 < steps else 1, cycle):
                    b_out(k, h, d).wait_send()
                if k + 1 < steps:
                    for other in range(chips):
                        c_out(k, h, other).wait_send()

            sent = lambda: others(far, lambda other: s_out(k, h, other).wait_send())
            if k + 1 < steps:
                pl.when(position != (k + 1) % cycle)(sent)
            else:
                sent()
            others(far, lambda other: s_pass(k, h, other).wait_send())
            s_pass(k, h, chip).wait_send()


def body(factor, loads):
    cycle = lax.axis_size("blk")
    places = lax.axis_size("rhs")
    rounds, _, share, width = factor.shape
    cases = loads.shape[3]
    block = share * places
    steps = width // block
    chips = places // 2
    dma = pltpu.SemaphoreType.DMA
    result = pl.pallas_call(
        functools.partial(kernel, (cycle, places, steps, rounds, share, block, cases)),
        out_shape=jax.ShapeDtypeStruct((rounds, share, cases), jnp.float32),
        in_specs=[pl.BlockSpec(memory_space=pl.ANY)] * 2,
        out_specs=pl.BlockSpec(memory_space=pltpu.VMEM),
        scratch_shapes=[
            pltpu.VMEM((rounds, steps, share, block), jnp.bfloat16),
            pltpu.VMEM((steps, 2, block // 2, cases), jnp.bfloat16),
            pltpu.VMEM((steps, 2, block // 2, cases), jnp.bfloat16),
            pltpu.VMEM((share, cases), jnp.float32),
            dma((rounds, steps)),
            dma,
            dma((steps, 2, places)),
            dma((steps, 2, places)),
            dma((steps, 2, chips)),
            dma((steps, 2, chips)),
            dma((steps, 2, cycle)),
            dma((steps, 2, chips)),
            dma((steps, 2, chips)),
            dma((steps, 2, chips)),
        ],
        compiler_params=pltpu.CompilerParams(
            collective_id=0, has_side_effects=True, vmem_limit_bytes=60 * 2**20),
    )(factor[:, 0], loads[:, 0])
    return result[:, None]


def solution(mesh):
    return jax.shard_map(
        body,
        mesh=mesh,
        in_specs=(P(None, "blk", "rhs", None), P(None, "blk", "rhs", None)),
        out_specs=P(None, "blk", "rhs", None),
        check_vma=False,
    )
```
